32 devices in a mesh: row: 8 (over y, x, core), col: 4 (over z).
Axes of the slice: x: 2, y: 2, z: 4, core: 2. Of those that a mesh axis runs over, the one named last changes fastest.
Arguments:
- a_tile: bfloat16 [2048, 16384], P('row', 'col'), may hold values from -6 to 6
- b_tile: bfloat16 [16384, 26624], P('row', 'col'), may hold values from -0.046875 to 0.046875
- c_prior: bfloat16 [2048, 26624], P('row', 'col'), may hold values from -0.29882812 to 0.29882812
- sketch_matrix: bfloat16 [26624, 128], P('col'), may hold values from -0.0390625 to 0.0390625
- panel_ids: int32 [2], replicated, may hold values from 0 to 31
Outputs:
- c_out: bfloat16 [2048, 26624], P('row', 'col')
- sketch: float32 [2048, 128], P('row')
- predicted: float32 [2048, 128], P('row')
The draws below stay inside these ranges and needn't reach their ends.
Inputs may be any that keep to these rules, and one draw needn't show every extreme that they name: `panel_ids`: the 2 ids may repeat.
All inputs are finite; a program needn't handle non-finite values.
Results may differ from the reference program's by a relative error of at most 0.0029.
Values may be sent and summed in bfloat16 or wider, within the bound.
No kernel may reach another device: no remote copies, remote signals or barrier semaphores. Data moves between devices by JAX's collectives and lax.ppermute only.
A program may use at most 128 MiB of HBM per device.

```python
import jax
import jax.numpy as jnp
from jax import lax

K = 16384
FF_W = 26624
PANEL = 512
STEPS = 2
SK = 128
TOKENS = 2048


def shard_levels(stream_key, dims, pieces, least, top_value):
    loudness = 1.0
    for dim, blocks in pieces:
        heights = jax.random.uniform(jax.random.fold_in(jax.random.fold_in(stream_key, 6), dim), (blocks,), jnp.float32, least / len(pieces), top_value / len(pieces))
        loudness = loudness * jnp.repeat(jnp.exp(heights), dims[dim] // blocks).reshape((-1,) + (1,) * (len(dims) - 1 - dim))
    return loudness


def normal_values(rng, extent, deviation, reach, split=(), held_as=jnp.bfloat16):
    drawn = jax.random.normal(rng, extent, jnp.float32) * deviation
    if len(split) > 0:
        drawn = shard_levels(rng, extent, split, -0.22, 0.18) * drawn
    return jnp.clip(drawn, min=-reach, max=reach).astype(held_as)


def setup_inputs(seed: int = 0) -> dict:
    key_of = jax.random.split(jax.random.key(seed), 6)
    a_tile = normal_values(key_of[0], (TOKENS, K), 1.0, 6.0, ((0, 8), (1, 4)))
    b_tile = normal_values(key_of[1], (K, FF_W), K ** -0.5, 0.046875, ((0, 8), (1, 4)))
    c_prior = normal_values(key_of[2], (TOKENS, FF_W), 0.05, 0.29882812, ((0, 8), (1, 4)))
    sketch_matrix = normal_values(key_of[3], (FF_W, SK), FF_W ** -0.5, 0.0390625, ((0, 4),))
    panel_ids = jax.random.randint(key_of[4], (STEPS,), 0, K // PANEL).astype(jnp.int32)
    return dict(a_tile=a_tile, b_tile=b_tile, c_prior=c_prior, sketch_matrix=sketch_matrix, panel_ids=panel_ids)


def reference(a_tile, b_tile, c_prior, sketch_matrix, panel_ids):
    running = c_prior.astype(jnp.float32)
    predicted = jnp.zeros((a_tile.shape[0], sketch_matrix.shape[1]), jnp.float32)
    for step in range(STEPS):
        first_row = (panel_ids[step] * PANEL).astype(jnp.int32)
        a_panel = lax.dynamic_slice_in_dim(a_tile, first_row, PANEL, 1)
        b_panel = lax.dynamic_slice_in_dim(b_tile, first_row, PANEL, 0)
        running = running + jnp.dot(a_panel, b_panel, preferred_element_type=jnp.float32)
        panel_sketch = jnp.dot(b_panel, sketch_matrix, preferred_element_type=jnp.float32)
        predicted = predicted + jnp.dot(a_panel.astype(jnp.float32), panel_sketch, precision=lax.Precision.HIGHEST)
    c_out = running.astype(jnp.bfloat16)
    sketch = jnp.dot(c_out, sketch_matrix, preferred_element_type=jnp.float32)
    return c_out, sketch, predicted
```

```python
import functools

import jax
import jax.numpy as jnp
from jax import lax
from jax.experimental import pallas as pl
from jax.experimental.pallas import tpu as pltpu
from jax.sharding import PartitionSpec as P

PANEL = 512
STEPS = 2
CORES = 2
LANES = 128
WIDTHS = (256, 256)
C_MOST = 3
HEAD = 2
LAST_PIECE = 4
PARTS = 2

ANY = pl.BlockSpec(memory_space=pl.ANY)
SMEM = pl.BlockSpec(memory_space=pltpu.SMEM)
VMEM = pl.BlockSpec(memory_space=pltpu.VMEM)


def broadcast(value, axis, source):
    kept = jnp.where(lax.axis_index(axis) == source, value, 0).astype(value.dtype)
    return lax.psum(kept, axis)


def plain(a_tile, b_tile, c_prior, sketch_matrix, panel_ids):
    running = c_prior.astype(jnp.float32)
    predicted = jnp.zeros((c_prior.shape[0], sketch_matrix.shape[1]), jnp.float32)
    for step in range(STEPS):
        first = panel_ids[step] * PANEL
        a_owner, a_first = first // a_tile.shape[1], first % a_tile.shape[1]
        b_owner, b_first = first // b_tile.shape[0], first % b_tile.shape[0]
        a_panel = broadcast(lax.dynamic_slice_in_dim(a_tile, a_first, PANEL, 1), "col", a_owner)
        b_panel = broadcast(lax.dynamic_slice_in_dim(b_tile, b_first, PANEL, 0), "row", b_owner)
        running = running + jnp.dot(a_panel, b_panel, preferred_element_type=jnp.float32)
        part = jnp.dot(b_panel, sketch_matrix, preferred_element_type=jnp.float32)
        predicted = predicted + jnp.dot(
            a_panel.astype(jnp.float32), part, precision=lax.Precision.HIGHEST
        )
    c_out = running.astype(jnp.bfloat16)
    sketch = jnp.dot(c_out, sketch_matrix, preferred_element_type=jnp.float32)
    sketch, predicted = lax.psum((sketch, predicted), "col")
    return c_out, sketch, predicted


OWN, NEAR, ROW, DIST, A_OWNER, A_FIRST = (STEPS * i for i in range(6))
CORE = STEPS * 6


def aligned(x, m):
    return pl.multiple_of(x, m)


def copy(src, dst, sem):
    return pltpu.make_async_copy(src, dst, sem)


def place_of(chip, n_chips):
    shift = 1
    out = chip
    while shift < n_chips:
        out = out ^ (chip >> shift)
        shift += 1
    return out


def panel_chunk(b_ref, scal, s, core, half, chunk):
    start, width = chunk
    rows = pl.ds(aligned(scal[ROW + s], PANEL), PANEL)
    return b_ref.at[rows, pl.ds(aligned(core * half + start, LANES), width)]


def stage(b_ref, scal, half, chains, outs, bufs, load_sem, store_sem):
    mine = scal[CORE]
    outs = list(outs)
    spots = []
    for c, chunks in enumerate(chains):
        for i, chunk in enumerate(chunks):
            for which in range(2):
                out = outs.pop(0)
                for s in range(STEPS):
                    spots.append(((which, i, s), c, chunk, out))
    spots.sort(key=lambda spot: (spot[0][0], spot[0][1]))

    def each(act):
        for spot, c, chunk, out in spots:
            core = mine if spot[0] else 1 - mine
            s = spot[2]
            load = lambda: copy(
                panel_chunk(b_ref, scal, s, core, half, chunk),
                bufs[c].at[spot],
                load_sem[c].at[spot],
            )
            store = lambda: copy(bufs[c].at[spot], out.at[s], store_sem[c].at[spot])

            @pl.when(scal[OWN + s] == 1)
            def _():
                act(load, store)

    def start(load, store):
        load().start()

    def turn(load, store):
        load().wait()
        store().start()

    def finish(load, store):
        store().wait()

    each(start)
    each(turn)
    each(finish)


def prologue_kernel(n_row, half, chains, ids, b_ref, a_ref, scal, cand, *rest):
    n = 2 * sum(len(chunks) for chunks in chains)
    outs = rest[:n]
    a_buf, a_sem = rest[n : n + 2]
    bufs, load_sem, store_sem = (rest[n + 2 + i :: 3] for i in range(3))
    n_chips = n_row // CORES
    me = lax.axis_index("row")
    core = lax.rem(me, CORES)
    chip = lax.div(me, CORES)
    scal[CORE] = core
    for s in range(STEPS):
        first = ids[s] * PANEL
        owner = lax.div(first, b_ref.shape[0])
        owner_chip = lax.div(owner, CORES)
        ahead = place_of(chip, n_chips) - place_of(owner_chip, n_chips)
        ahead = jnp.where(core == 0, ahead, -ahead)
        scal[OWN + s] = (owner == me).astype(jnp.int32)
        scal[NEAR + s] = ((owner_chip == chip) & (owner != me)).astype(jnp.int32)
        scal[ROW + s] = lax.rem(first, b_ref.shape[0])
        scal[DIST + s] = jnp.where(ahead < 0, ahead + n_chips, ahead)
        scal[A_OWNER + s] = lax.div(first, a_ref.shape[1])
        scal[A_FIRST + s] = lax.rem(first, a_ref.shape[1])

    def a_load(s):
        cols = pl.ds(aligned(scal[A_FIRST + s], PANEL), PANEL)
        return copy(a_ref.at[:, cols], a_buf.at[:, pl.ds(s * PANEL, PANEL)], a_sem.at[s])

    for s in range(STEPS):
        a_load(s).start()
    stage(b_ref, scal, half, chains, outs, bufs, load_sem, store_sem)
    for s in range(STEPS):
        a_load(s).wait()
    out = copy(a_buf, cand, a_sem.at[0])
    out.start()
    out.wait()


def stage_kernel(half, chains, scal, b_ref, tok_in, *rest):
    n = 2 * sum(len(chunks) for chunks in chains)
    outs, rest = rest[:n], rest[n + 1 :]
    stage(b_ref, scal, half, chains, outs, *(rest[i::3] for i in range(3)))


def inject_kernel(first, done, scal, *refs):
    if done:
        return
    refs = list(refs)
    if not first:
        refs.pop(0)
    sib, own, tok_in, out, tok_out, buf, load_sem, store_sem = refs
    rows = PANEL // PARTS
    for act in ("load", "turn", "finish"):
        for flag, source in ((OWN, own), (NEAR, sib)):
            for s in range(STEPS):

                @pl.when(scal[flag + s] == 1)
                def _(source=source, s=s, act=act):
                    for p in range(PARTS):
                        part = pl.ds(p * rows, rows)
                        spot = (s, part)
                        load = lambda: copy(source.at[spot], buf.at[spot], load_sem.at[s, p])
                        store = lambda: copy(buf.at[spot], out.at[spot], store_sem.at[s, p])
                        if act == "load":
                            load().start()
                        elif act == "turn":
                            load().wait()
                            store().start()
                        else:
                            store().wait()


def pick_kernel(n_col, k, panels, scal, *refs):
    cand, out, tok_out, sem = refs[0], *refs[-3:]
    z = lax.axis_index("col")
    for i, s in enumerate(panels):
        away = z - scal[A_OWNER + s]
        away = jnp.where(away < 0, away + n_col, away)

        @pl.when(away == k)
        def _(i=i, s=s):
            cp = copy(
                cand.at[:, pl.ds(i * PANEL, PANEL)], out.at[:, pl.ds(s * PANEL, PANEL)], sem
            )
            cp.start()
            cp.wait()


def split3(x):
    hi = x.astype(jnp.bfloat16)
    rest = x - hi.astype(jnp.float32)
    mid = rest.astype(jnp.bfloat16)
    lo = (rest - mid.astype(jnp.float32)).astype(jnp.bfloat16)
    return hi, mid, lo


def fdot(a, b):
    return jnp.dot(a, b, preferred_element_type=jnp.float32)


def work_kernel(plan, ring, half, *refs):
    p_chunks, c_chunks, back, firsts, last = plan
    refs = list(refs)
    take = lambda n: [refs.pop(0) for _ in range(n)]
    scal, s_ref = take(2)
    chunks = sorted(set(p_chunks) | set(c_chunks))
    cands = {c: take(ring) for c in chunks}
    (tok_in,) = take(1)
    ps_in = None if firsts[0] else take(1)[0]
    if c_chunks or last:
        (a_ref,) = take(1)
    if c_chunks:
        c_ref, c_sib = take(2)
        sk_in, cout_in = (None, None) if firsts[1] else take(2)
        gots = take(len(back))
    tok_out, ps = take(2)
    if c_chunks:
        sk, cout = take(2)
        rets = take(len(c_chunks))
    b_buf, s_buf, c_buf, b_sem, s_sem, c_sem, o_sem, g_sem = take(8)
    mine = scal[CORE] * half
    theirs = (1 - scal[CORE]) * half
    rows = c_buf.shape[1] // CORES

    def load_b(i, s, which):
        width = chunks[i][1]
        return copy(
            cands[chunks[i]][which].at[s],
            b_buf.at[i, pl.ds(s * PANEL, PANEL), pl.ds(0, width)],
            b_sem.at[i, s],
        )

    def load_s(i):
        start, width = chunks[i]
        cols = pl.ds(aligned(mine + start, LANES), width)
        return copy(s_ref.at[cols, :], s_buf.at[i, pl.ds(0, width)], s_sem.at[i])

    def load_c(i):
        start, width = c_chunks[i]
        part = pl.ds(0, width)
        return (
            copy(
                c_ref.at[:, pl.ds(aligned(mine + start, LANES), width)],
                c_buf.at[i, pl.ds(0, rows), part],
                c_sem.at[i, 0],
            ),
            copy(
                c_sib.at[:, pl.ds(start, width)],
                c_buf.at[i, pl.ds(rows, rows), part],
                c_sem.at[i, 1],
            ),
        )

    def store_c(i):
        start, width = c_chunks[i]
        return copy(
            c_buf.at[i, pl.ds(0, rows), pl.ds(0, width)],
            cout.at[:, pl.ds(aligned(mine + start, LANES), width)],
            o_sem.at[i],
        )

    def store_got(i):
        start, width = back[i]
        return copy(
            gots[i], cout.at[:, pl.ds(aligned(theirs + start, LANES), width)], g_sem.at[i]
        )

    for i in range(len(chunks)):
        for s in range(STEPS):
            for which in range(ring):

                @pl.when(scal[DIST + s] == which)
                def _(i=i, s=s, which=which):
                    load_b(i, s, which).start()

        load_s(i).start()
    for i in range(len(c_chunks)):
        for cp in load_c(i):
            cp.start()
    for i in range(len(back)):
        store_got(i).start()
    if firsts[0]:
        ps[...] = jnp.zeros_like(ps)
    else:
        ps[...] = ps_in[...]
    if c_chunks:
        if firsts[1]:
            sk[...] = jnp.zeros_like(sk)
        else:
            sk[...] = sk_in[...]
    for i, chunk in enumerate(chunks):
        width = chunk[1]
        for s in range(STEPS):
            load_b(i, s, 0).wait()
        load_s(i).wait()
        b = b_buf[i, :, :width]
        sm = s_buf[i, :width, :]
        if chunk in c_chunks:
            k = c_chunks.index(chunk)
            for cp in load_c(k):
                cp.wait()
            c = c_buf[k, :, :width].astype(jnp.float32) + fdot(a_ref[...], b)
            c = c.astype(jnp.bfloat16)
            c_buf[k, :, :width] = c
            rets[k][...] = c[rows:]
            store_c(k).start()
            sk[...] += fdot(c, sm)
        if chunk in p_chunks:
            ps[...] += fdot(b, sm)
    if last:
        hi, mid, lo = split3(ps[...])
        a = a_ref[...]
        ps[: CORES * rows, :] = fdot(a, hi) + (fdot(a, mid) + fdot(a, lo))
    for i in range(len(c_chunks)):
        store_c(i).wait()
    for i in range(len(back)):
        store_got(i).wait()


def place_kernel(back, half, scal, *refs):
    gots, cout, sem = refs[: len(back)], refs[-2], refs[-1]
    theirs = (1 - scal[CORE]) * half
    copies = [
        copy(got, cout.at[:, pl.ds(aligned(theirs + start, LANES), width)], sem.at[i])
        for i, (got, (start, width)) in enumerate(zip(gots, back))
    ]
    for cp in copies:
        cp.start()
    for cp in copies:
        cp.wait()


def like(shape, dtype=jnp.bfloat16):
    return jax.ShapeDtypeStruct(shape, dtype)


def params(mb):
    return pltpu.CompilerParams(vmem_limit_bytes=mb * 2**20)


def call(kernel, **kw):
    cost = pl.CostEstimate(flops=1, bytes_accessed=1, transcendentals=0)
    return pl.pallas_call(kernel, cost_estimate=cost, **kw)


DMA = pltpu.SemaphoreType.DMA


def ring_form(n_row, n_col, a_tile, b_tile, c_prior, sketch_matrix, panel_ids):
    rows, wide = c_prior.shape
    half = wide // CORES
    sk_cols = sketch_matrix.shape[1]
    n_chips = n_row // CORES
    order = [i ^ (i >> 1) for i in range(n_chips)]
    place = [order.index(c) for c in range(n_chips)]
    follow = [order[(place[c] + 1) % n_chips] for c in range(n_chips)]
    before = [order[(place[c] - 1) % n_chips] for c in range(n_chips)]
    around = []
    for c in range(n_chips):
        around += [(CORES * c, CORES * follow[c]), (CORES * c + 1, CORES * before[c] + 1)]
    swap = [(d, d ^ 1) for d in range(n_row)]

    def spread(x):
        return lax.ppermute(x, "row", around)

    def exchange(x):
        return lax.ppermute(x, "row", swap)

    chains = [[] for _ in WIDTHS]
    at = turn = 0
    while at < half:
        width = WIDTHS[turn % len(WIDTHS)]
        if at + width > half:
            turn += 1
            continue
        chains[turn % len(WIDTHS)].append((at, width))
        at += width
        turn += 1
    n_chains = len(chains)
    heads = [chunks[:HEAD] for chunks in chains]
    tails = [chunks[HEAD:] for chunks in chains]

    def staged(parts):
        shapes, specs = [], []
        for chunks, width in zip(parts, WIDTHS):
            shapes += [like((STEPS, PANEL, width))] * (2 * len(chunks))
            specs += [ANY] * (2 * len(chunks))
        return tuple(shapes), tuple(specs)

    def unpack(arrays, parts):
        arrays = list(arrays)
        return [
            [(exchange(arrays.pop(0)), arrays.pop(0)) for _ in chunks] for chunks in parts
        ]

    def stage_scratch(parts):
        out = []
        for chunks, width in zip(parts, WIDTHS):
            n = len(chunks)
            out += [
                pltpu.VMEM((2, n, STEPS, PANEL, width), jnp.bfloat16),
                DMA((2, n, STEPS)),
                DMA((2, n, STEPS)),
            ]
        return out

    scal, cand, *staged_heads = call(
        functools.partial(prologue_kernel, n_row, half, heads),
        out_shape=(like((CORE + 1,), jnp.int32), like((rows, STEPS * PANEL))) + staged(heads)[0],
        in_specs=[SMEM, ANY, ANY],
        out_specs=(SMEM, ANY) + staged(heads)[1],
        scratch_shapes=[pltpu.VMEM((rows, STEPS * PANEL), jnp.bfloat16), DMA((STEPS,))]
        + stage_scratch(heads),
        compiler_params=params(62),
    )(panel_ids, b_tile, a_tile)

    feeds = unpack(staged_heads, heads)
    tok = jnp.zeros((8, LANES), jnp.float32)

    def inject(tok, c, t, recv, feed):
        first = recv is None
        args = [scal] + ([] if first else [recv]) + ([] if feed is None else list(feed)) + [tok]
        aliases = {} if first else {1: 0}
        return call(
            functools.partial(inject_kernel, first, feed is None),
            out_shape=(like((STEPS, PANEL, WIDTHS[c])), like(tok.shape, tok.dtype)),
            in_specs=[SMEM] + [ANY] * (len(args) - 1),
            out_specs=(ANY, ANY),
            scratch_shapes=[
                pltpu.VMEM((STEPS, PANEL, WIDTHS[c]), jnp.bfloat16),
                DMA((STEPS, PARTS)),
                DMA((STEPS, PARTS)),
            ],
            input_output_aliases=aliases,
            compiler_params=params(4),
        )(*args)

    sends = [[] for _ in chains]
    flying = [None] * n_chains
    for c in range(n_chains):
        sent, tok = inject(tok, c, 0, None, feeds[c][0])
        sends[c].append(sent)
        flying[c] = spread(sent)
    def pick(tok, k, panels, piece, mine):
        args = [scal, piece] + ([] if mine is None else [mine]) + [tok]
        return call(
            functools.partial(pick_kernel, n_col, k, panels),
            out_shape=(like(cand.shape), like(tok.shape, tok.dtype)),
            in_specs=[SMEM, ANY] + ([] if mine is None else [VMEM]) + [ANY],
            out_specs=(VMEM, ANY),
            scratch_shapes=[DMA],
            input_output_aliases={} if mine is None else {2: 0},
            compiler_params=params(4),
        )(*args)

    a_own, tok = pick(tok, 0, tuple(range(STEPS)), cand, None)
    c_other = exchange(
        lax.dynamic_slice_in_dim(c_prior, (1 - lax.axis_index("row") % CORES) * half, half, 1)
    )
    a_all = None
    pieces = []
    for k in sorted(range(1, n_col), key=lambda k: min(k, n_col - k)):
        if 2 * k == n_col:
            pieces += [(k, (s,)) for s in range(STEPS)]
        else:
            pieces.append((k, tuple(range(STEPS))))

    state = dict(ps=None, sk=None, cout=None, waiting=[])

    def work(tok, p_ids, c_ids, last=False):
        where = lambda cj: chains[cj[0]][cj[1]]
        p_chunks = [where(cj) for cj in p_ids]
        c_chunks = [where(cj) for cj in c_ids]
        ids = sorted(set(p_ids) | set(c_ids), key=where)
        n = len(ids)
        widest = max(where(cj)[1] for cj in ids)
        firsts = (state["ps"] is None, state["sk"] is None)
        back = []
        if c_ids:
            while len(state["waiting"]) > 2:
                back.append(state["waiting"].pop(0))
        args = [scal, sketch_matrix]
        specs = [SMEM, ANY]
        for c, j in ids:
            args += sends[c][j : j + n_chips]
            specs += [ANY] * n_chips
        aliases = {}
        args.append(tok)
        specs.append(ANY)
        outs = [like(tok.shape, tok.dtype), like((STEPS * PANEL, sk_cols), jnp.float32)]
        out_specs = [ANY, VMEM]
        if not firsts[0]:
            aliases[len(args)] = 1
            args.append(state["ps"])
            specs.append(VMEM)
        if c_ids or last:
            args.append(a_all)
            specs.append(VMEM)
        if c_ids:
            args += [c_prior, c_other]
            specs += [ANY, ANY]
            if not firsts[1]:
                aliases[len(args)] = 2
                aliases[len(args) + 1] = 3
                args += [state["sk"], state["cout"]]
                specs += [VMEM, ANY]
            args += [got for got, _ in back]
            specs += [VMEM] * len(back)
            outs += [like((CORES * rows, sk_cols), jnp.float32), like((rows, wide))]
            out_specs += [VMEM, ANY]
            outs += [like((rows, w)) for _, w in c_chunks]
            out_specs += [VMEM] * len(c_chunks)
        m = max(1, len(c_ids))
        plan = (p_chunks, c_chunks, [spot for _, spot in back], firsts, last)
        got = call(
            functools.partial(work_kernel, plan, n_chips, half),
            out_shape=tuple(outs),
            in_specs=specs,
            out_specs=tuple(out_specs),
            scratch_shapes=[
                pltpu.VMEM((n, STEPS * PANEL, widest), jnp.bfloat16),
                pltpu.VMEM((n, widest, sk_cols), jnp.bfloat16),
                pltpu.VMEM((m, CORES * rows, widest), jnp.bfloat16),
                DMA((n, STEPS)),
                DMA((n,)),
                DMA((m, CORES)),
                DMA((m,)),
                DMA((max(1, len(back)),)),
            ],
            input_output_aliases=aliases,
            compiler_params=params(16),
        )(*args)
        tok, state["ps"] = got[:2]
        if c_ids:
            state["sk"], state["cout"] = got[2:4]
            for ret, spot in zip(got[4:], c_chunks):
                state["waiting"].append((exchange(ret), spot))
        return tok

    p_todo, c_todo = [], []
    n_steps = [len(chunks) + n_chips - 2 for chunks in chains]
    for t in range(1, max(n_steps) + 1):
        if t == HEAD - 1:
            *staged_tails, tok = call(
                functools.partial(stage_kernel, half, tails),
                out_shape=staged(tails)[0] + (like(tok.shape, tok.dtype),),
                in_specs=[SMEM, ANY, ANY],
                out_specs=staged(tails)[1] + (ANY,),
                scratch_shapes=stage_scratch(tails),
                compiler_params=params(62),
            )(scal, b_tile, tok)
            feeds = [old + new for old, new in zip(feeds, unpack(staged_tails, tails))]
        for c in range(n_chains):
            if t > n_steps[c]:
                continue
            if t < len(chains[c]):
                sent, tok = inject(tok, c, t, flying[c], feeds[c][t])
            elif t < n_steps[c]:
                sent, tok = inject(tok, c, t, flying[c], None)
            else:
                sent = flying[c]
            sends[c].append(sent)
            if t < n_steps[c]:
                flying[c] = spread(sent)
            if t >= n_chips - 1:
                p_todo.append((c, t - n_chips + 1))
                c_todo.append((c, t - n_chips + 1))
            if c == n_chains - 1 and a_all is None:
                for k, panels in pieces[:1] if t < LAST_PIECE else pieces:
                    way = [(i, (i + k) % n_col) for i in range(n_col)]
                    piece = cand
                    if len(panels) == 1:
                        piece = cand[:, panels[0] * PANEL : (panels[0] + 1) * PANEL]
                    a_own, tok = pick(tok, k, panels, lax.ppermute(piece, "col", way), a_own)
                pieces = pieces[1:] if t < LAST_PIECE else []
                if not pieces:
                    a_all = jnp.concatenate([a_own, exchange(a_own)], 0)
            if t == max(n_steps) and all(len(sends[k]) > n_steps[k] for k in range(n_chains)):
                continue
            c_ids = c_todo[:C_MOST] if a_all is not None else []
            if c < n_chains - 1 and t <= min(n_steps):
                continue
            if p_todo or c_ids:
                tok = work(tok, p_todo, c_ids)
                p_todo, c_todo = [], c_todo[len(c_ids) :]
    tok = work(tok, p_todo, c_todo, True)

    back = state["waiting"]
    cout = call(
        functools.partial(place_kernel, [spot for _, spot in back], half),
        out_shape=like((rows, wide)),
        in_specs=[SMEM] + [VMEM] * len(back) + [ANY],
        out_specs=ANY,
        scratch_shapes=[DMA((len(back),))],
        input_output_aliases={len(back) + 1: 0},
        compiler_params=params(4),
    )(scal, *[got for got, _ in back], state["cout"])

    sk, ps = state["sk"], state["ps"]
    mine = jnp.concatenate([sk[:rows], ps[:rows]], 1)
    theirs = exchange(jnp.concatenate([sk[rows:], ps[rows : 2 * rows]], 1))
    total = mine + theirs
    z = lax.axis_index("col")
    share = rows // n_col
    shift = lambda k: [(i, (i + k) % n_col) for i in range(n_col)]
    cut = lambda i: lax.dynamic_slice_in_dim(total, (i % n_col) * share, share, 0)
    part = cut(z)
    for k in range(1, n_col):
        part = part + lax.ppermute(cut(z + k), "col", shift(k))
    full = jnp.zeros_like(total)
    full = lax.dynamic_update_slice_in_dim(full, part, z * share, 0)
    for k in range(1, n_col):
        full = lax.dynamic_update_slice_in_dim(
            full, lax.ppermute(part, "col", shift(k)), ((z - k) % n_col) * share, 0
        )
    return cout, full[:, :sk_cols], full[:, sk_cols:]


def solution(mesh):
    n_row, n_col = mesh.shape["row"], mesh.shape["col"]

    def per_device(a_tile, b_tile, c_prior, sketch_matrix, panel_ids):
        rows, wide = c_prior.shape
        chips = n_row // CORES
        fits = (
            n_row == CORES * chips
            and chips & (chips - 1) == 0
            and chips > 1
            and wide % (CORES * LANES) == 0
            and wide // CORES >= 4 * sum(WIDTHS)
            and (wide // CORES) % min(WIDTHS) == 0
            and b_tile.shape[0] % PANEL == 0
            and a_tile.shape[1] % PANEL == 0
            and CORES * rows <= STEPS * PANEL
            and rows % (8 * n_col) == 0
        )
        if not fits:
            return plain(a_tile, b_tile, c_prior, sketch_matrix, panel_ids)
        return ring_form(n_row, n_col, a_tile, b_tile, c_prior, sketch_matrix, panel_ids)

    placed = (P("row", "col"), P("row", "col"), P("row", "col"), P("col", None), P())
    return jax.shard_map(
        per_device,
        mesh=mesh,
        in_specs=placed,
        out_specs=(P("row", "col"), P("row", None), P("row", None)),
        check_vma=False,
    )
```

```python
import functools

import jax
import jax.numpy as jnp
from jax import lax
from jax.experimental import pallas as pl
from jax.experimental.pallas import tpu as pltpu
from jax.sharding import PartitionSpec as P

PANEL = 512
STEPS = 2
CORES = 2
LANES = 128
WIDTHS = (256, 256)
C_MOST = 3
HOPS = (1, 0), (2, 1), (4, 0)
PARTS = 2

ANY = pl.BlockSpec(memory_space=pl.ANY)
SMEM = pl.BlockSpec(memory_space=pltpu.SMEM)
VMEM = pl.BlockSpec(memory_space=pltpu.VMEM)


def broadcast(value, axis, source):
    kept = jnp.where(lax.axis_index(axis) == source, value, 0).astype(value.dtype)
    return lax.psum(kept, axis)


def plain(a_tile, b_tile, c_prior, sketch_matrix, panel_ids):
    running = c_prior.astype(jnp.float32)
    predicted = jnp.zeros((c_prior.shape[0], sketch_matrix.shape[1]), jnp.float32)
    for step in range(STEPS):
        first = panel_ids[step] * PANEL
        a_owner, a_first = first // a_tile.shape[1], first % a_tile.shape[1]
        b_owner, b_first = first // b_tile.shape[0], first % b_tile.shape[0]
        a_panel = broadcast(lax.dynamic_slice_in_dim(a_tile, a_first, PANEL, 1), "col", a_owner)
        b_panel = broadcast(lax.dynamic_slice_in_dim(b_tile, b_first, PANEL, 0), "row", b_owner)
        running = running + jnp.dot(a_panel, b_panel, preferred_element_type=jnp.float32)
        part = jnp.dot(b_panel, sketch_matrix, preferred_element_type=jnp.float32)
        predicted = predicted + jnp.dot(
            a_panel.astype(jnp.float32), part, precision=lax.Precision.HIGHEST
        )
    c_out = running.astype(jnp.bfloat16)
    sketch = jnp.dot(c_out, sketch_matrix, preferred_element_type=jnp.float32)
    sketch, predicted = lax.psum((sketch, predicted), "col")
    return c_out, sketch, predicted


OWN, NEAR, ROW, DIST, A_OWNER = (STEPS * i for i in range(5))
CORE = STEPS * 5


def aligned(x, m):
    return pl.multiple_of(x, m)


def copy(src, dst, sem):
    return pltpu.make_async_copy(src, dst, sem)


def place_of(chip, n_chips):
    shift = 1
    out = chip
    while shift < n_chips:
        out = out ^ (chip >> shift)
        shift += 1
    return out


def panel_chunk(b_ref, scal, s, core, half, chunk):
    start, width = chunk
    rows = pl.ds(aligned(scal[ROW + s], PANEL), PANEL)
    return b_ref.at[rows, pl.ds(aligned(core * half + start, LANES), width)]


def prologue_kernel(n_row, half, chunks, ids, b_ref, a_ref, scal, cand, tok_out, *rest):
    n = len(chunks)
    outs, (a_buf, bufs, a_sem, load_sem, store_sem) = rest[:n], rest[n:]
    n_chips = n_row // CORES
    me = lax.axis_index("row")
    core = lax.rem(me, CORES)
    chip = lax.div(me, CORES)
    scal[CORE] = core
    for s in range(STEPS):
        first = ids[s] * PANEL
        owner = lax.div(first, b_ref.shape[0])
        owner_chip = lax.div(owner, CORES)
        ahead = place_of(chip, n_chips) - place_of(owner_chip, n_chips)
        ahead = jnp.where(core == 0, ahead, -ahead)
        scal[OWN + s] = (owner == me).astype(jnp.int32)
        scal[NEAR + s] = ((owner_chip == chip) & (owner != me)).astype(jnp.int32)
        scal[ROW + s] = lax.rem(first, b_ref.shape[0])
        scal[DIST + s] = jnp.where(ahead < 0, ahead + n_chips, ahead)
        scal[A_OWNER + s] = lax.div(first, a_ref.shape[1])

    def a_load(s):
        first = lax.rem(ids[s] * PANEL, a_ref.shape[1])
        cols = pl.ds(aligned(first, PANEL), PANEL)
        return copy(a_ref.at[:, cols], a_buf.at[:, pl.ds(s * PANEL, PANEL)], a_sem.at[s])

    def each(act):
        for i, chunk in enumerate(chunks):
            for s in range(STEPS):
                load = lambda: copy(
                    panel_chunk(b_ref, scal, s, 1 - core, half, chunk),
                    bufs.at[i, s, :, pl.ds(0, chunk[1])],
                    load_sem.at[i, s],
                )
                store = lambda: copy(
                    bufs.at[i, s, :, pl.ds(0, chunk[1])], outs[i].at[s], store_sem.at[i, s]
                )

                @pl.when(scal[OWN + s] == 1)
                def _():
                    act(load, store)

    owner = scal[OWN] + scal[OWN + 1] > 0

    @pl.when(owner)
    def _():
        each(lambda load, store: load().start())

    for s in range(STEPS):
        a_load(s).start()

    @pl.when(owner)
    def _():
        def turn(load, store):
            load().wait()
            store().start()

        each(turn)

    for s in range(STEPS):
        a_load(s).wait()
    out = copy(a_buf, cand, a_sem.at[0])
    out.start()

    @pl.when(owner)
    def _():
        each(lambda load, store: store().wait())

    out.wait()


def take_panels(n_col, hop, scal, came, held, buf, sem, act):
    z = lax.axis_index("col")
    mid = n_col // 2
    for s in range(STEPS):
        owner = scal[A_OWNER + s]
        outer = jnp.where(lax.rem(z + 1, n_col) < 2, 1, 0)
        apart = jnp.where(lax.div(z, mid) == lax.div(owner, mid), 0, 1)
        other = jnp.where(owner == z, 0, 1)
        take = ((1 - outer) * (1 - apart) * other, (1 - outer) * apart, outer * other)[hop]

        @pl.when(take == 1)
        def _(s=s):
            cols = pl.ds(s * PANEL, PANEL)
            load = lambda: copy(came.at[:, cols], buf.at[:, cols], sem.at[0, s])
            store = lambda: copy(buf.at[:, cols], held.at[:, cols], sem.at[1, s])
            if act == "load":
                load().start()
            elif act == "turn":
                load().wait()
                store().start()
            else:
                store().wait()


def inject_kernel(n_col, half, chunk, first, hop, scal, *refs):
    refs = list(refs)
    take = lambda n: [refs.pop(0) for _ in range(n)]
    if not first:
        take(1)
    if chunk is not None:
        b_ref, sib = take(2)
    if hop is not None:
        came, held_in = take(2)
    tok_in, out, tok_out = take(3)
    if hop is not None:
        (held,) = take(1)
    buf, load_sem, store_sem, a_buf, a_sem = refs
    rows = PANEL // PARTS
    for act in ("load", "turn", "finish"):
        if hop is not None:
            take_panels(n_col, hop, scal, came, held, a_buf, a_sem, act)
        if chunk is None:
            continue
        for flag in (OWN, NEAR):
            for s in range(STEPS):

                @pl.when(scal[flag + s] == 1)
                def _(flag=flag, s=s, act=act):
                    if flag == OWN:
                        source = panel_chunk(b_ref, scal, s, scal[CORE], half, chunk)
                    else:
                        source = sib.at[s]
                    for p in range(PARTS):
                        part = pl.ds(p * rows, rows)
                        spot = (s, part)
                        load = lambda: copy(source.at[part], buf.at[spot], load_sem.at[s, p])
                        store = lambda: copy(buf.at[spot], out.at[spot], store_sem.at[s, p])
                        if act == "load":
                            load().start()
                        elif act == "turn":
                            load().wait()
                            store().start()
                        else:
                            store().wait()


def share_kernel(half, scal, c_ref, tok_in, out, tok_out, buf, sem):
    cols = pl.ds(aligned((1 - scal[CORE]) * half, LANES), half)
    for one, two in ((c_ref.at[:, cols], buf), (buf, out)):
        cp = copy(one, two, sem)
        cp.start()
        cp.wait()


def split3(x):
    hi = x.astype(jnp.bfloat16)
    rest = x - hi.astype(jnp.float32)
    mid = rest.astype(jnp.bfloat16)
    lo = (rest - mid.astype(jnp.float32)).astype(jnp.bfloat16)
    return hi, mid, lo


def fdot(a, b):
    return jnp.dot(a, b, preferred_element_type=jnp.float32)


def work_kernel(plan, ring, half, *refs):
    p_chunks, c_chunks, back, firsts, last = plan
    refs = list(refs)
    take = lambda n: [refs.pop(0) for _ in range(n)]
    scal, s_ref = take(2)
    chunks = sorted(set(p_chunks) | set(c_chunks))
    cands = {c: take(ring) for c in chunks}
    (tok_in,) = take(1)
    ps_in = None if firsts[0] else take(1)[0]
    if c_chunks or last:
        a_refs = take(2)
    if c_chunks:
        c_ref, c_sib = take(2)
        sk_in, cout_in = (None, None) if firsts[1] else take(2)
        gots = take(len(back))
    tok_out, ps = take(2)
    if c_chunks:
        sk, cout = take(2)
        rets = take(len(c_chunks))
    totals = take(2) if last else []
    b_buf, s_buf, c_buf, b_sem, s_sem, c_sem, o_sem, g_sem = take(8)
    mine = scal[CORE] * half
    theirs = (1 - scal[CORE]) * half
    rows = c_buf.shape[1] // CORES

    def load_b(i, s, which):
        width = chunks[i][1]
        return copy(
            cands[chunks[i]][which].at[s],
            b_buf.at[i, pl.ds(s * PANEL, PANEL), pl.ds(0, width)],
            b_sem.at[i, s],
        )

    def load_s(i):
        start, width = chunks[i]
        cols = pl.ds(aligned(mine + start, LANES), width)
        return copy(s_ref.at[cols, :], s_buf.at[i, pl.ds(0, width)], s_sem.at[i])

    def load_c(i):
        start, width = c_chunks[i]
        part = pl.ds(0, width)
        return (
            copy(
                c_ref.at[:, pl.ds(aligned(mine + start, LANES), width)],
                c_buf.at[i, pl.ds(0, rows), part],
                c_sem.at[i, 0],
            ),
            copy(
                c_sib.at[:, pl.ds(start, width)],
                c_buf.at[i, pl.ds(rows, rows), part],
                c_sem.at[i, 1],
            ),
        )

    def store_c(i):
        start, width = c_chunks[i]
        return copy(
            c_buf.at[i, pl.ds(0, rows), pl.ds(0, width)],
            cout.at[:, pl.ds(aligned(mine + start, LANES), width)],
            o_sem.at[i],
        )

    def store_got(i):
        start, width = back[i]
        return copy(
            gots[i], cout.at[:, pl.ds(aligned(theirs + start, LANES), width)], g_sem.at[i]
        )

    for i in range(len(chunks)):
        for s in range(STEPS):
            for which in range(ring):

                @pl.when(scal[DIST + s] == which)
                def _(i=i, s=s, which=which):
                    load_b(i, s, which).start()

        load_s(i).start()
    for i in range(len(c_chunks)):
        for cp in load_c(i):
            cp.start()
    for i in range(len(back)):
        store_got(i).start()
    if firsts[0]:
        ps[...] = jnp.zeros_like(ps)
    else:
        ps[...] = ps_in[...]
    if c_chunks:
        if firsts[1]:
            sk[...] = jnp.zeros_like(sk)
        else:
            sk[...] = sk_in[...]
    for i, chunk in enumerate(chunks):
        width = chunk[1]
        for s in range(STEPS):
            load_b(i, s, 0).wait()
        load_s(i).wait()
        b = b_buf[i, :, :width]
        sm = s_buf[i, :width, :]
        if chunk in c_chunks:
            k = c_chunks.index(chunk)
            for cp in load_c(k):
                cp.wait()
            for h, a_ref in enumerate(a_refs):
                part = slice(h * rows, (h + 1) * rows)
                c = c_buf[k, part, :width].astype(jnp.float32) + fdot(a_ref[...], b)
                c = c.astype(jnp.bfloat16)
                if h == 0:
                    c_buf[k, part, :width] = c
                    store_c(k).start()
                else:
                    rets[k][...] = c
                sk[part, :] += fdot(c, sm)
        if chunk in p_chunks:
            ps[...] += fdot(b, sm)
    if last:
        hi, mid, lo = split3(ps[...])
        cols = sk.shape[1]
        for h, (a_ref, total) in enumerate(zip(a_refs, totals)):
            a = a_ref[...]
            total[:, :cols] = sk[h * rows : (h + 1) * rows, :]
            total[:, cols:] = fdot(a, hi) + (fdot(a, mid) + fdot(a, lo))
    for i in range(len(c_chunks)):
        store_c(i).wait()
    for i in range(len(back)):
        store_got(i).wait()


def place_kernel(back, half, scal, *refs):
    gots, cout, sem = refs[: len(back)], refs[-2], refs[-1]
    theirs = (1 - scal[CORE]) * half
    copies = [
        copy(got, cout.at[:, pl.ds(aligned(theirs + start, LANES), width)], sem.at[i])
        for i, (got, (start, width)) in enumerate(zip(gots, back))
    ]
    for cp in copies:
        cp.start()
    for cp in copies:
        cp.wait()


def like(shape, dtype=jnp.bfloat16):
    return jax.ShapeDtypeStruct(shape, dtype)


def params(mb):
    return pltpu.CompilerParams(vmem_limit_bytes=mb * 2**20)


def call(kernel, **kw):
    cost = pl.CostEstimate(flops=1, bytes_accessed=1, transcendentals=0)
    return pl.pallas_call(kernel, cost_estimate=cost, **kw)


DMA = pltpu.SemaphoreType.DMA


def ring_form(n_row, n_col, a_tile, b_tile, c_prior, sketch_matrix, panel_ids):
    rows, wide = c_prior.shape
    half = wide // CORES
    sk_cols = sketch_matrix.shape[1]
    n_chips = n_row // CORES
    order = [i ^ (i >> 1) for i in range(n_chips)]
    place = [order.index(c) for c in range(n_chips)]
    follow = [order[(place[c] + 1) % n_chips] for c in range(n_chips)]
    before = [order[(place[c] - 1) % n_chips] for c in range(n_chips)]
    around = []
    for c in range(n_chips):
        around += [(CORES * c, CORES * follow[c]), (CORES * c + 1, CORES * before[c] + 1)]
    swap = [(d, d ^ 1) for d in range(n_row)]

    def spread(x):
        return lax.ppermute(x, "row", around)

    def exchange(x):
        return lax.ppermute(x, "row", swap)

    chains = [[] for _ in WIDTHS]
    at = turn = 0
    while at < half:
        width = WIDTHS[turn % len(WIDTHS)]
        if at + width > half:
            turn += 1
            continue
        chains[turn % len(WIDTHS)].append((at, width))
        at += width
        turn += 1
    n_chains = len(chains)
    order_of = sorted(
        ((j, c) for c in range(n_chains) for j in range(len(chains[c])))
    )
    flat = [chains[c][j] for j, c in order_of]
    widest = max(WIDTHS)
    scal, cand, tok, *others = call(
        functools.partial(prologue_kernel, n_row, half, flat),
        out_shape=(
            like((CORE + 1,), jnp.int32),
            like((rows, STEPS * PANEL)),
            like((8, LANES)),
        )
        + tuple(like((STEPS, PANEL, width)) for _, width in flat),
        in_specs=[SMEM, ANY, ANY],
        out_specs=(SMEM,) + (ANY,) * (2 + len(flat)),
        scratch_shapes=[
            pltpu.VMEM((rows, STEPS * PANEL), jnp.bfloat16),
            pltpu.VMEM((len(flat), STEPS, PANEL, widest), jnp.bfloat16),
            DMA((STEPS,)),
            DMA((len(flat), STEPS)),
            DMA((len(flat), STEPS)),
        ],
        compiler_params=params(62),
    )(panel_ids, b_tile, a_tile)
    sibs = {(c, j): exchange(other) for (j, c), other in zip(order_of, others)}

    mid = n_col // 2
    hops = [[(i, i + 1) for i in range(mid - 1)] + [(i, i - 1) for i in range(mid + 1, n_col)]]
    hops.append([(mid - 1, mid), (mid, mid - 1)])
    hops.append([(j, i) for i, j in hops[0]])

    def inject(tok, c, t, recv, hop=None, cand=None):
        chunk = chains[c][t] if t < len(chains[c]) else None
        first = recv is None
        args = [scal] + ([] if first else [recv])
        aliases = {} if first else {1: 0}
        if chunk is not None:
            args += [b_tile, sibs[c, t]]
        outs = [like((STEPS, PANEL, WIDTHS[c])), like(tok.shape, tok.dtype)]
        if hop is not None:
            aliases[len(args) + 1] = 2
            args += [lax.ppermute(cand, "col", hops[hop]), cand]
            outs.append(like(cand.shape))
        args.append(tok)
        return call(
            functools.partial(inject_kernel, n_col, half, chunk, first, hop),
            out_shape=tuple(outs),
            in_specs=[SMEM] + [ANY] * (len(args) - 1),
            out_specs=(ANY,) * len(outs),
            scratch_shapes=[
                pltpu.VMEM((STEPS, PANEL, WIDTHS[c]), jnp.bfloat16),
                DMA((STEPS, PARTS)),
                DMA((STEPS, PARTS)),
                pltpu.VMEM((rows, STEPS * PANEL), jnp.bfloat16),
                DMA((2, STEPS)),
            ],
            input_output_aliases=aliases,
            compiler_params=params(40),
        )(*args)

    sends = [[] for _ in chains]
    flying = [None] * n_chains
    for c in range(n_chains):
        sent, tok = inject(tok, c, 0, None)
        sends[c].append(sent)
        flying[c] = spread(sent)

    c_other, tok = call(
        functools.partial(share_kernel, half),
        out_shape=(like((rows, half)), like(tok.shape, tok.dtype)),
        in_specs=[SMEM, ANY, ANY],
        out_specs=(ANY, ANY),
        scratch_shapes=[pltpu.VMEM((rows, half), jnp.bfloat16), DMA],
        compiler_params=params(4),
    )(scal, c_prior, tok)
    c_other = exchange(c_other)

    state = dict(ps=None, sk=None, cout=None, waiting=[])

    def work(tok, c_ids, last=False):
        p_ids = c_ids
        where = lambda cj: chains[cj[0]][cj[1]]
        p_chunks = [where(cj) for cj in p_ids]
        c_chunks = [where(cj) for cj in c_ids]
        ids = sorted(set(p_ids) | set(c_ids), key=where)
        n = len(ids)
        widest = max(where(cj)[1] for cj in ids)
        firsts = (state["ps"] is None, state["sk"] is None)
        back = []
        if c_ids:
            while len(state["waiting"]) > 2:
                back.append(state["waiting"].pop(0))
        args = [scal, sketch_matrix]
        specs = [SMEM, ANY]
        for c, j in ids:
            args += sends[c][j : j + n_chips]
            specs += [ANY] * n_chips
        aliases = {}
        args.append(tok)
        specs.append(ANY)
        outs = [like(tok.shape, tok.dtype), like((STEPS * PANEL, sk_cols), jnp.float32)]
        out_specs = [ANY, VMEM]
        if not firsts[0]:
            aliases[len(args)] = 1
            args.append(state["ps"])
            specs.append(VMEM)
        if c_ids or last:
            args += a_all
            specs += [VMEM, VMEM]
        if c_ids:
            args += [c_prior, c_other]
            specs += [ANY, ANY]
            if not firsts[1]:
                aliases[len(args)] = 2
                aliases[len(args) + 1] = 3
                args += [state["sk"], state["cout"]]
                specs += [VMEM, ANY]
            args += [got for got, _ in back]
            specs += [VMEM] * len(back)
            outs += [like((CORES * rows, sk_cols), jnp.float32), like((rows, wide))]
            out_specs += [VMEM, ANY]
            outs += [like((rows, w)) for _, w in c_chunks]
            out_specs += [VMEM] * len(c_chunks)
        if last:
            outs += [like((rows, 2 * sk_cols), jnp.float32)] * 2
            out_specs += [VMEM] * 2
        m = max(1, len(c_ids))
        plan = (p_chunks, c_chunks, [spot for _, spot in back], firsts, last)
        got = call(
            functools.partial(work_kernel, plan, n_chips, half),
            out_shape=tuple(outs),
            in_specs=specs,
            out_specs=tuple(out_specs),
            scratch_shapes=[
                pltpu.VMEM((n, STEPS * PANEL, widest), jnp.bfloat16),
                pltpu.VMEM((n, widest, sk_cols), jnp.bfloat16),
                pltpu.VMEM((m, CORES * rows, widest), jnp.bfloat16),
                DMA((n, STEPS)),
                DMA((n,)),
                DMA((m, CORES)),
                DMA((m,)),
                DMA((max(1, len(back)),)),
            ],
            input_output_aliases=aliases,
            compiler_params=params(16),
        )(*args)
        tok, state["ps"] = got[:2]
        if c_ids:
            state["sk"], state["cout"] = got[2:4]
            state["totals"] = got[4 + len(c_chunks) :]
            for ret, spot in zip(got[4:], c_chunks):
                state["waiting"].append((exchange(ret), spot))
        return tok

    c_todo = []
    n_steps = [len(chunks) + n_chips - 2 for chunks in chains]
    for t in range(1, max(n_steps) + 1):
        for c in range(n_chains):
            if t > n_steps[c]:
                continue
            if (t, c) in HOPS:
                sent, tok, cand = inject(tok, c, t, flying[c], HOPS.index((t, c)), cand)
                if (t, c) == HOPS[-1]:
                    a_all = cand, exchange(cand)
            elif t < n_steps[c]:
                sent, tok = inject(tok, c, t, flying[c])
            else:
                sent = flying[c]
            sends[c].append(sent)
            if t < n_steps[c]:
                flying[c] = spread(sent)
            if t >= n_chips - 1:
                c_todo.append((c, t - n_chips + 1))
            if t == max(n_steps) and all(len(sends[k]) > n_steps[k] for k in range(n_chains)):
                continue
            c_ids = c_todo[:C_MOST] if t >= HOPS[-1][0] else []
            if c < n_chains - 1 and t <= min(n_steps):
                continue
            if c_ids:
                tok = work(tok, c_ids)
                c_todo = c_todo[len(c_ids) :]
    tok = work(tok, c_todo, True)

    back = state["waiting"]
    cout = call(
        functools.partial(place_kernel, [spot for _, spot in back], half),
        out_shape=like((rows, wide)),
        in_specs=[SMEM] + [VMEM] * len(back) + [ANY],
        out_specs=ANY,
        scratch_shapes=[DMA((len(back),))],
        input_output_aliases={len(back) + 1: 0},
        compiler_params=params(4),
    )(scal, *[got for got, _ in back], state["cout"])

    mine, theirs = state["totals"]
    total = mine + exchange(theirs)
    z = lax.axis_index("col")
    share = rows // n_col
    shift = lambda k: [(i, (i + k) % n_col) for i in range(n_col)]
    cut = lambda i: lax.dynamic_slice_in_dim(total, (i % n_col) * share, share, 0)
    part = cut(z)
    for k in range(1, n_col):
        part = part + lax.ppermute(cut(z + k), "col", shift(k))
    full = jnp.zeros_like(total)
    full = lax.dynamic_update_slice_in_dim(full, part, z * share, 0)
    for k in range(1, n_col):
        full = lax.dynamic_update_slice_in_dim(
            full, lax.ppermute(part, "col", shift(k)), ((z - k) % n_col) * share, 0
        )
    return cout, full[:, :sk_cols], full[:, sk_cols:]


def solution(mesh):
    n_row, n_col = mesh.shape["row"], mesh.shape["col"]

    def per_device(a_tile, b_tile, c_prior, sketch_matrix, panel_ids):
        rows, wide = c_prior.shape
        chips = n_row // CORES
        fits = (
            n_row == CORES * chips
            and chips & (chips - 1) == 0
            and chips > 1
            and wide % (CORES * LANES) == 0
            and wide // CORES >= 4 * sum(WIDTHS)
            and (wide // CORES) % min(WIDTHS) == 0
            and b_tile.shape[0] % PANEL == 0
            and a_tile.shape[1] % PANEL == 0
            and CORES * rows <= STEPS * PANEL
            and rows % (8 * n_col) == 0
            and n_col == 4
        )
        if not fits:
            return plain(a_tile, b_tile, c_prior, sketch_matrix, panel_ids)
        return ring_form(n_row, n_col, a_tile, b_tile, c_prior, sketch_matrix, panel_ids)

    placed = (P("row", "col"), P("row", "col"), P("row", "col"), P("col", None), P())
    return jax.shard_map(
        per_device,
        mesh=mesh,
        in_specs=placed,
        out_specs=(P("row", "col"), P("row", None), P("row", None)),
        check_vma=False,
    )
```

```python
import functools

import jax
import jax.numpy as jnp
from jax import lax
from jax.experimental import pallas as pl
from jax.experimental.pallas import tpu as pltpu
from jax.sharding import PartitionSpec as P

PANEL = 512
STEPS = 2
CORES = 2
LANES = 128
WIDTHS = (256, 256)
C_MOST = 4
HOPS = (1, 0), (2, 1), (4, 0)
PARTS = 1

ANY = pl.BlockSpec(memory_space=pl.ANY)
SMEM = pl.BlockSpec(memory_space=pltpu.SMEM)
VMEM = pl.BlockSpec(memory_space=pltpu.VMEM)


def broadcast(value, axis, source):
    kept = jnp.where(lax.axis_index(axis) == source, value, 0).astype(value.dtype)
    return lax.psum(kept, axis)


def plain(a_tile, b_tile, c_prior, sketch_matrix, panel_ids):
    running = c_prior.astype(jnp.float32)
    predicted = jnp.zeros((c_prior.shape[0], sketch_matrix.shape[1]), jnp.float32)
    for step in range(STEPS):
        first = panel_ids[step] * PANEL
        a_owner, a_first = first // a_tile.shape[1], first % a_tile.shape[1]
        b_owner, b_first = first // b_tile.shape[0], first % b_tile.shape[0]
        a_panel = broadcast(lax.dynamic_slice_in_dim(a_tile, a_first, PANEL, 1), "col", a_owner)
        b_panel = broadcast(lax.dynamic_slice_in_dim(b_tile, b_first, PANEL, 0), "row", b_owner)
        running = running + jnp.dot(a_panel, b_panel, preferred_element_type=jnp.float32)
        part = jnp.dot(b_panel, sketch_matrix, preferred_element_type=jnp.float32)
        predicted = predicted + jnp.dot(
            a_panel.astype(jnp.float32), part, precision=lax.Precision.HIGHEST
        )
    c_out = running.astype(jnp.bfloat16)
    sketch = jnp.dot(c_out, sketch_matrix, preferred_element_type=jnp.float32)
    sketch, predicted = lax.psum((sketch, predicted), "col")
    return c_out, sketch, predicted


OWN, NEAR, ROW, DIST, A_OWNER = (STEPS * i for i in range(5))
CORE = STEPS * 5


def aligned(x, m):
    return pl.multiple_of(x, m)


def copy(src, dst, sem):
    return pltpu.make_async_copy(src, dst, sem)


def place_of(chip, n_chips):
    shift = 1
    out = chip
    while shift < n_chips:
        out = out ^ (chip >> shift)
        shift += 1
    return out


def panel_chunk(b_ref, scal, s, core, half, chunk):
    start, width = chunk
    rows = pl.ds(aligned(scal[ROW + s], PANEL), PANEL)
    return b_ref.at[rows, pl.ds(aligned(core * half + start, LANES), width)]


def prologue_kernel(n_row, half, chunks, ids, b_ref, a_ref, scal, cand, *rest):
    n = len(chunks)
    outs, (a_buf, bufs, a_sem, load_sem, store_sem) = rest[:n], rest[n:]
    n_chips = n_row // CORES
    me = lax.axis_index("row")
    core = lax.rem(me, CORES)
    chip = lax.div(me, CORES)
    scal[CORE] = core
    for s in range(STEPS):
        first = ids[s] * PANEL
        owner = lax.div(first, b_ref.shape[0])
        owner_chip = lax.div(owner, CORES)
        ahead = place_of(chip, n_chips) - place_of(owner_chip, n_chips)
        ahead = jnp.where(core == 0, ahead, -ahead)
        scal[OWN + s] = (owner == me).astype(jnp.int32)
        scal[NEAR + s] = ((owner_chip == chip) & (owner != me)).astype(jnp.int32)
        scal[ROW + s] = lax.rem(first, b_ref.shape[0])
        scal[DIST + s] = jnp.where(ahead < 0, ahead + n_chips, ahead)
        scal[A_OWNER + s] = lax.div(first, a_ref.shape[1])

    def a_load(s):
        first = lax.rem(ids[s] * PANEL, a_ref.shape[1])
        cols = pl.ds(aligned(first, PANEL), PANEL)
        return copy(a_ref.at[:, cols], a_buf.at[:, pl.ds(s * PANEL, PANEL)], a_sem.at[s])

    def each(act):
        for i, chunk in enumerate(chunks):
            for s in range(STEPS):
                load = lambda: copy(
                    panel_chunk(b_ref, scal, s, 1 - core, half, chunk),
                    bufs.at[i, s, :, pl.ds(0, chunk[1])],
                    load_sem.at[i, s],
                )
                store = lambda: copy(
                    bufs.at[i, s, :, pl.ds(0, chunk[1])], outs[i].at[s], store_sem.at[i, s]
                )

                @pl.when(scal[OWN + s] == 1)
                def _():
                    act(load, store)

    owner = scal[OWN] + scal[OWN + 1] > 0

    @pl.when(owner)
    def _():
        each(lambda load, store: load().start())

    for s in range(STEPS):
        a_load(s).start()

    @pl.when(owner)
    def _():
        def turn(load, store):
            load().wait()
            store().start()

        each(turn)

    for s in range(STEPS):
        a_load(s).wait()
    out = copy(a_buf, cand, a_sem.at[0])
    out.start()

    @pl.when(owner)
    def _():
        each(lambda load, store: store().wait())

    out.wait()


def take_panels(n_col, hop, scal, came, held, buf, sem, act):
    z = lax.axis_index("col")
    mid = n_col // 2
    for s in range(STEPS):
        owner = scal[A_OWNER + s]
        outer = jnp.where(lax.rem(z + 1, n_col) < 2, 1, 0)
        apart = jnp.where(lax.div(z, mid) == lax.div(owner, mid), 0, 1)
        other = jnp.where(owner == z, 0, 1)
        take = ((1 - outer) * (1 - apart) * other, (1 - outer) * apart, outer * other)[hop]

        @pl.when(take == 1)
        def _(s=s):
            cols = pl.ds(s * PANEL, PANEL)
            load = lambda: copy(came.at[:, cols], buf.at[:, cols], sem.at[0, s])
            store = lambda: copy(buf.at[:, cols], held.at[:, cols], sem.at[1, s])
            if act == "load":
                load().start()
            elif act == "turn":
                load().wait()
                store().start()
            else:
                store().wait()


def inject_kernel(n_col, half, chunk, first, alone, hop, scal, *refs):
    refs = list(refs)
    take = lambda n: [refs.pop(0) for _ in range(n)]
    if not first:
        take(1)
    if chunk is not None:
        b_ref, sib = take(2)
    if hop is not None:
        came, held_in = take(2)
    if not first or not alone:
        take(1)
    out, tok_out = take(2)
    if hop is not None:
        (held,) = take(1)
    buf, load_sem, store_sem, a_buf, a_sem = refs
    rows = PANEL // PARTS
    for act in ("load", "turn", "finish"):
        if hop is not None:
            take_panels(n_col, hop, scal, came, held, a_buf, a_sem, act)
        if chunk is None:
            continue
        for flag in (OWN, NEAR):
            for s in range(STEPS):

                @pl.when(scal[flag + s] == 1)
                def _(flag=flag, s=s, act=act):
                    if flag == OWN:
                        source = panel_chunk(b_ref, scal, s, scal[CORE], half, chunk)
                    else:
                        source = sib.at[s]
                    for p in range(PARTS):
                        part = pl.ds(p * rows, rows)
                        spot = (s, part)
                        load = lambda: copy(source.at[part], buf.at[spot], load_sem.at[s, p])
                        store = lambda: copy(buf.at[spot], out.at[spot], store_sem.at[s, p])
                        if act == "load":
                            load().start()
                        elif act == "turn":
                            load().wait()
                            store().start()
                        else:
                            store().wait()


def share_kernel(half, scal, c_ref, tok_in, out, tok_out, buf, sem):
    cols = pl.ds(aligned((1 - scal[CORE]) * half, LANES), half)
    for one, two in ((c_ref.at[:, cols], buf), (buf, out)):
        cp = copy(one, two, sem)
        cp.start()
        cp.wait()


def split3(x):
    hi = x.astype(jnp.bfloat16)
    rest = x - hi.astype(jnp.float32)
    mid = rest.astype(jnp.bfloat16)
    lo = (rest - mid.astype(jnp.float32)).astype(jnp.bfloat16)
    return hi, mid, lo


def fdot(a, b):
    return jnp.dot(a, b, preferred_element_type=jnp.float32)


def work_kernel(plan, ring, half, *refs):
    p_chunks, c_chunks, back, firsts, last = plan
    refs = list(refs)
    take = lambda n: [refs.pop(0) for _ in range(n)]
    scal, s_ref = take(2)
    chunks = sorted(set(p_chunks) | set(c_chunks))
    cands = {c: take(ring) for c in chunks}
    (tok_in,) = take(1)
    ps_in = None if firsts[0] else take(1)[0]
    if c_chunks or last:
        a_refs = take(2)
    if c_chunks:
        c_ref, c_sib = take(2)
        sk_in, cout_in = (None, None) if firsts[1] else take(2)
        gots = take(len(back))
    tok_out, ps = take(2)
    if c_chunks:
        sk, cout = take(2)
        rets = take(len(c_chunks))
    totals = take(2) if last else []
    b_buf, s_buf, c_buf, b_sem, s_sem, c_sem, o_sem, g_sem = take(8)
    mine = scal[CORE] * half
    theirs = (1 - scal[CORE]) * half
    rows = c_buf.shape[1] // CORES

    def load_b(i, s, which):
        width = chunks[i][1]
        return copy(
            cands[chunks[i]][which].at[s],
            b_buf.at[i, pl.ds(s * PANEL, PANEL), pl.ds(0, width)],
            b_sem.at[i, s],
        )

    def load_s(i):
        start, width = chunks[i]
        cols = pl.ds(aligned(mine + start, LANES), width)
        return copy(s_ref.at[cols, :], s_buf.at[i, pl.ds(0, width)], s_sem.at[i])

    def load_c(i):
        start, width = c_chunks[i]
        part = pl.ds(0, width)
        return (
            copy(
                c_ref.at[:, pl.ds(aligned(mine + start, LANES), width)],
                c_buf.at[i, pl.ds(0, rows), part],
                c_sem.at[i, 0],
            ),
            copy(
                c_sib.at[:, pl.ds(start, width)],
                c_buf.at[i, pl.ds(rows, rows), part],
                c_sem.at[i, 1],
            ),
        )

    def store_c(i):
        start, width = c_chunks[i]
        return copy(
            c_buf.at[i, pl.ds(0, rows), pl.ds(0, width)],
            cout.at[:, pl.ds(aligned(mine + start, LANES), width)],
            o_sem.at[i],
        )

    def store_got(i):
        start, width = back[i]
        return copy(
            gots[i], cout.at[:, pl.ds(aligned(theirs + start, LANES), width)], g_sem.at[i]
        )

    for i in range(len(chunks)):
        for s in range(STEPS):
            for which in range(ring):

                @pl.when(scal[DIST + s] == which)
                def _(i=i, s=s, which=which):
                    load_b(i, s, which).start()

        load_s(i).start()
    for i in range(len(c_chunks)):
        for cp in load_c(i):
            cp.start()
    for i in range(len(back)):
        store_got(i).start()
    if firsts[0]:
        ps[...] = jnp.zeros_like(ps)
    else:
        ps[...] = ps_in[...]
    if c_chunks:
        if firsts[1]:
            sk[...] = jnp.zeros_like(sk)
        else:
            sk[...] = sk_in[...]
    for i, chunk in enumerate(chunks):
        width = chunk[1]
        for s in range(STEPS):
            load_b(i, s, 0).wait()
        load_s(i).wait()
        b = b_buf[i, :, :width]
        sm = s_buf[i, :width, :]
        if chunk in c_chunks:
            k = c_chunks.index(chunk)
            for cp in load_c(k):
                cp.wait()
            for h, a_ref in enumerate(a_refs):
                part = slice(h * rows, (h + 1) * rows)
                c = c_buf[k, part, :width].astype(jnp.float32) + fdot(a_ref[...], b)
                c = c.astype(jnp.bfloat16)
                if h == 0:
                    c_buf[k, part, :width] = c
                    store_c(k).start()
                else:
                    rets[k][...] = c
                sk[part, :] += fdot(c, sm)
        if chunk in p_chunks:
            ps[...] += fdot(b, sm)
    if last:
        hi, mid, lo = split3(ps[...])
        cols = sk.shape[1]
        for h, (a_ref, total) in enumerate(zip(a_refs, totals)):
            a = a_ref[...]
            total[:, :cols] = sk[h * rows : (h + 1) * rows, :]
            total[:, cols:] = fdot(a, hi) + (fdot(a, mid) + fdot(a, lo))
    for i in range(len(c_chunks)):
        store_c(i).wait()
    for i in range(len(back)):
        store_got(i).wait()


def place_kernel(back, half, scal, *refs):
    gots, cout, sem = refs[: len(back)], refs[-2], refs[-1]
    theirs = (1 - scal[CORE]) * half
    copies = [
        copy(got, cout.at[:, pl.ds(aligned(theirs + start, LANES), width)], sem.at[i])
        for i, (got, (start, width)) in enumerate(zip(gots, back))
    ]
    for cp in copies:
        cp.start()
    for cp in copies:
        cp.wait()


def like(shape, dtype=jnp.bfloat16):
    return jax.ShapeDtypeStruct(shape, dtype)


def params(mb):
    return pltpu.CompilerParams(vmem_limit_bytes=mb * 2**20)


def call(kernel, **kw):
    cost = pl.CostEstimate(flops=1, bytes_accessed=1, transcendentals=0)
    return pl.pallas_call(kernel, cost_estimate=cost, **kw)


DMA = pltpu.SemaphoreType.DMA


def ring_form(n_row, n_col, a_tile, b_tile, c_prior, sketch_matrix, panel_ids):
    rows, wide = c_prior.shape
    half = wide // CORES
    sk_cols = sketch_matrix.shape[1]
    n_chips = n_row // CORES
    order = [i ^ (i >> 1) for i in range(n_chips)]
    place = [order.index(c) for c in range(n_chips)]
    follow = [order[(place[c] + 1) % n_chips] for c in range(n_chips)]
    before = [order[(place[c] - 1) % n_chips] for c in range(n_chips)]
    around = []
    for c in range(n_chips):
        around += [(CORES * c, CORES * follow[c]), (CORES * c + 1, CORES * before[c] + 1)]
    swap = [(d, d ^ 1) for d in range(n_row)]

    def spread(x):
        return lax.ppermute(x, "row", around)

    def exchange(x):
        return lax.ppermute(x, "row", swap)

    chains = [[] for _ in WIDTHS]
    at = turn = 0
    while at < half:
        width = WIDTHS[turn % len(WIDTHS)]
        if at + width > half:
            turn += 1
            continue
        chains[turn % len(WIDTHS)].append((at, width))
        at += width
        turn += 1
    n_chains = len(chains)
    order_of = sorted(
        ((j, c) for c in range(n_chains) for j in range(len(chains[c])))
    )
    flat = [chains[c][j] for j, c in order_of]
    widest = max(WIDTHS)
    scal, cand, *others = call(
        functools.partial(prologue_kernel, n_row, half, flat),
        out_shape=(
            like((CORE + 1,), jnp.int32),
            like((rows, STEPS * PANEL)),
        )
        + tuple(like((STEPS, PANEL, width)) for _, width in flat),
        in_specs=[SMEM, ANY, ANY],
        out_specs=(SMEM,) + (ANY,) * (1 + len(flat)),
        scratch_shapes=[
            pltpu.VMEM((rows, STEPS * PANEL), jnp.bfloat16),
            pltpu.VMEM((len(flat), STEPS, PANEL, widest), jnp.bfloat16),
            DMA((STEPS,)),
            DMA((len(flat), STEPS)),
            DMA((len(flat), STEPS)),
        ],
        compiler_params=params(62),
    )(panel_ids, b_tile, a_tile)
    sibs = {(c, j): exchange(other) for (j, c), other in zip(order_of, others)}

    mid = n_col // 2
    hops = [[(i, i + 1) for i in range(mid - 1)] + [(i, i - 1) for i in range(mid + 1, n_col)]]
    hops.append([(mid - 1, mid), (mid, mid - 1)])
    hops.append([(j, i) for i, j in hops[0]])

    def inject(tok, c, t, recv, hop=None, cand=None):
        chunk = chains[c][t] if t < len(chains[c]) else None
        first = recv is None
        args = [scal] + ([] if first else [recv])
        aliases = {} if first else {1: 0}
        if chunk is not None:
            args += [b_tile, sibs[c, t]]
        outs = [like((STEPS, PANEL, WIDTHS[c])), like((8, LANES))]
        if hop is not None:
            aliases[len(args) + 1] = 2
            args += [lax.ppermute(cand, "col", hops[hop]), cand]
            outs.append(like(cand.shape))
        if tok is not None:
            args.append(tok)
        return call(
            functools.partial(inject_kernel, n_col, half, chunk, first, tok is None, hop),
            out_shape=tuple(outs),
            in_specs=[SMEM] + [ANY] * (len(args) - 1),
            out_specs=(ANY,) * len(outs),
            scratch_shapes=[
                pltpu.VMEM((STEPS, PANEL, WIDTHS[c]), jnp.bfloat16),
                DMA((STEPS, PARTS)),
                DMA((STEPS, PARTS)),
                pltpu.VMEM((rows, STEPS * PANEL), jnp.bfloat16),
                DMA((2, STEPS)),
            ],
            input_output_aliases=aliases,
            compiler_params=params(40),
        )(*args)

    sends = [[] for _ in chains]
    tok = None
    flying = [None] * n_chains
    for c in range(n_chains):
        sent, tok = inject(tok, c, 0, None)
        sends[c].append(sent)
        flying[c] = spread(sent)

    c_other, tok = call(
        functools.partial(share_kernel, half),
        out_shape=(like((rows, half)), like(tok.shape, tok.dtype)),
        in_specs=[SMEM, ANY, ANY],
        out_specs=(ANY, ANY),
        scratch_shapes=[pltpu.VMEM((rows, half), jnp.bfloat16), DMA],
        compiler_params=params(4),
    )(scal, c_prior, tok)
    c_other = exchange(c_other)

    state = dict(ps=None, sk=None, cout=None, waiting=[])

    def work(tok, c_ids, last=False):
        p_ids = c_ids
        where = lambda cj: chains[cj[0]][cj[1]]
        p_chunks = [where(cj) for cj in p_ids]
        c_chunks = [where(cj) for cj in c_ids]
        ids = sorted(set(p_ids) | set(c_ids), key=where)
        n = len(ids)
        widest = max(where(cj)[1] for cj in ids)
        firsts = (state["ps"] is None, state["sk"] is None)
        back = []
        if c_ids:
            while len(state["waiting"]) > 2:
                back.append(state["waiting"].pop(0))
        args = [scal, sketch_matrix]
        specs = [SMEM, ANY]
        for c, j in ids:
            args += sends[c][j : j + n_chips]
            specs += [ANY] * n_chips
        aliases = {}
        args.append(tok)
        specs.append(ANY)
        outs = [like(tok.shape, tok.dtype), like((STEPS * PANEL, sk_cols), jnp.float32)]
        out_specs = [ANY, VMEM]
        if not firsts[0]:
            aliases[len(args)] = 1
            args.append(state["ps"])
            specs.append(VMEM)
        if c_ids or last:
            args += a_all
            specs += [VMEM, VMEM]
        if c_ids:
            args += [c_prior, c_other]
            specs += [ANY, ANY]
            if not firsts[1]:
                aliases[len(args)] = 2
                aliases[len(args) + 1] = 3
                args += [state["sk"], state["cout"]]
                specs += [VMEM, ANY]
            args += [got for got, _ in back]
            specs += [VMEM] * len(back)
            outs += [like((CORES * rows, sk_cols), jnp.float32), like((rows, wide))]
            out_specs += [VMEM, ANY]
            outs += [like((rows, w)) for _, w in c_chunks]
            out_specs += [VMEM] * len(c_chunks)
        if last:
            outs += [like((rows, 2 * sk_cols), jnp.float32)] * 2
            out_specs += [VMEM] * 2
        m = max(1, len(c_ids))
        plan = (p_chunks, c_chunks, [spot for _, spot in back], firsts, last)
        got = call(
            functools.partial(work_kernel, plan, n_chips, half),
            out_shape=tuple(outs),
            in_specs=specs,
            out_specs=tuple(out_specs),
            scratch_shapes=[
                pltpu.VMEM((n, STEPS * PANEL, widest), jnp.bfloat16),
                pltpu.VMEM((n, widest, sk_cols), jnp.bfloat16),
                pltpu.VMEM((m, CORES * rows, widest), jnp.bfloat16),
                DMA((n, STEPS)),
                DMA((n,)),
                DMA((m, CORES)),
                DMA((m,)),
                DMA((max(1, len(back)),)),
            ],
            input_output_aliases=aliases,
            compiler_params=params(16),
        )(*args)
        tok, state["ps"] = got[:2]
        if c_ids:
            state["sk"], state["cout"] = got[2:4]
            state["totals"] = got[4 + len(c_chunks) :]
            for ret, spot in zip(got[4:], c_chunks):
                state["waiting"].append((exchange(ret), spot))
        return tok

    c_todo = []
    n_steps = [len(chunks) + n_chips - 2 for chunks in chains]
    for t in range(1, max(n_steps) + 1):
        for c in range(n_chains):
            if t > n_steps[c]:
                continue
            if (t, c) in HOPS:
                sent, tok, cand = inject(tok, c, t, flying[c], HOPS.index((t, c)), cand)
                if (t, c) == HOPS[-1]:
                    a_all = cand, exchange(cand)
            elif t < n_steps[c]:
                sent, tok = inject(tok, c, t, flying[c])
            else:
                sent = flying[c]
            sends[c].append(sent)
            if t < n_steps[c]:
                flying[c] = spread(sent)
            if t >= n_chips - 1:
                c_todo.append((c, t - n_chips + 1))
            if t == max(n_steps) and all(len(sends[k]) > n_steps[k] for k in range(n_chains)):
                continue
            c_ids = c_todo[:C_MOST] if t >= HOPS[-1][0] else []
            if c < n_chains - 1 and t <= min(n_steps):
                continue
            if c_ids:
                tok = work(tok, c_ids)
                c_todo = c_todo[len(c_ids) :]
    tok = work(tok, c_todo, True)

    back = state["waiting"]
    cout = call(
        functools.partial(place_kernel, [spot for _, spot in back], half),
        out_shape=like((rows, wide)),
        in_specs=[SMEM] + [VMEM] * len(back) + [ANY],
        out_specs=ANY,
        scratch_shapes=[DMA((len(back),))],
        input_output_aliases={len(back) + 1: 0},
        compiler_params=params(4),
    )(scal, *[got for got, _ in back], state["cout"])

    mine, theirs = state["totals"]
    total = mine + exchange(theirs)
    z = lax.axis_index("col")
    share = rows // n_col
    shift = lambda k: [(i, (i + k) % n_col) for i in range(n_col)]
    cut = lambda i: lax.dynamic_slice_in_dim(total, (i % n_col) * share, share, 0)
    part = cut(z)
    for k in range(1, n_col):
        part = part + lax.ppermute(cut(z + k), "col", shift(k))
    full = jnp.zeros_like(total)
    full = lax.dynamic_update_slice_in_dim(full, part, z * share, 0)
    for k in range(1, n_col):
        full = lax.dynamic_update_slice_in_dim(
            full, lax.ppermute(part, "col", shift(k)), ((z - k) % n_col) * share, 0
        )
    return cout, full[:, :sk_cols], full[:, sk_cols:]


def solution(mesh):
    n_row, n_col = mesh.shape["row"], mesh.shape["col"]

    def per_device(a_tile, b_tile, c_prior, sketch_matrix, panel_ids):
        rows, wide = c_prior.shape
        chips = n_row // CORES
        fits = (
            n_row == CORES * chips
            and chips & (chips - 1) == 0
            and chips > 1
            and wide % (CORES * LANES) == 0
            and wide // CORES >= 4 * sum(WIDTHS)
            and (wide // CORES) % min(WIDTHS) == 0
            and b_tile.shape[0] % PANEL == 0
            and a_tile.shape[1] % PANEL == 0
            and CORES * rows <= STEPS * PANEL
            and rows % (8 * n_col) == 0
            and n_col == 4
        )
        if not fits:
            return plain(a_tile, b_tile, c_prior, sketch_matrix, panel_ids)
        return ring_form(n_row, n_col, a_tile, b_tile, c_prior, sketch_matrix, panel_ids)

    placed = (P("row", "col"), P("row", "col"), P("row", "col"), P("col", None), P())
    return jax.shard_map(
        per_device,
        mesh=mesh,
        in_specs=placed,
        out_specs=(P("row", "col"), P("row", None), P("row", None)),
        check_vma=False,
    )
```
